512 devices in a mesh: blk: 128 (over x, z_lo, y), heads: 4 (over z_hi, core).
Axes of the slice: x: 4, y: 8, z: 8 (z_hi: 2, z_lo: 4; z = z_hi * 4 + z_lo), core: 2. Of those that a mesh axis runs over, the one named last changes fastest.
Arguments:
- queries: bfloat16 [32768, 4096], P('blk', 'heads'), may hold values from -5 to 5
- keys: bfloat16 [32768, 1024], P('blk', 'heads'), may hold values from -5 to 5
- values: bfloat16 [32768, 1024], P('blk', 'heads'), may hold values from -6 to 6
- doc_ids: int32 [32768], P('blk'), may hold values from 0 to 127, never falling along the last dimension, each value on 1 to 1024 neighbouring positions
Outputs:
- attended: bfloat16 [32768, 4096], P('blk', 'heads')
The draws below stay inside these ranges and needn't reach their ends.
Inputs may be any that keep to these rules, and one draw needn't show every extreme that they name: `doc_ids`: Non-decreasing along the sequence; every document has 1024 tokens at most, and some document exactly 1024.
All inputs are finite; a program needn't handle non-finite values.
Results may differ from the reference program's by a relative error of at most 0.0034.
Values may be sent and summed in bfloat16 or wider, within the bound.
No kernel may reach another device: no remote copies, remote signals or barrier semaphores. Data moves between devices by JAX's collectives and lax.ppermute only.
A program may use at most 64 MiB of HBM per device.

```python
import math
import jax
import jax.numpy as jnp
import numpy as np
from jax import lax

QUERY_HEAD_COUNT = 32
KEY_VALUE_HEADS = 8
HEAD_WIDTH = 128
BLOCK_TOKENS = 256
DOC_BLKS = 4
MAXDOC = 1024
PACKED_TOKENS = 32768
DOCS = 128


def make_pair(key):
    start_offset = jax.random.fold_in(key, 7)
    key_portion = jnp.clip(jax.random.normal(jax.random.fold_in(start_offset, 1), (PACKED_TOKENS, KEY_VALUE_HEADS * HEAD_WIDTH), jnp.float32), -4.0, 4.0)
    query_part = jnp.clip(jax.random.normal(jax.random.fold_in(start_offset, 2), (PACKED_TOKENS, QUERY_HEAD_COUNT * HEAD_WIDTH), jnp.float32), -4.0, 4.0)
    return (query_part, key_portion)


def draw_queries(key, part):
    return make_pair(key)[0].astype(jnp.bfloat16)


def draw_keys(key, part):
    return make_pair(key)[1].astype(jnp.bfloat16)


def block_levels(own_key, shape, cuts, smallest, high):
    loudness = 1.0
    for dim, parts in cuts:
        draws = jax.random.uniform(jax.random.fold_in(jax.random.fold_in(own_key, 6), dim), (parts,), jnp.float32, smallest / len(cuts), high / len(cuts))
        loudness = loudness * jnp.repeat(jnp.exp(draws), shape[dim] // parts).reshape((-1,) + (1,) * (len(shape) - 1 - dim))
    return loudness


def profile(count, total, limit, slope):
    loads = [(1 << 20) // math.isqrt(standing ** slope) + 1 for standing in range(2, count + 1)]
    surplus, counts = total - limit - (count - 1), [1] * (count - 1)
    while surplus > 0:
        movable = [i for i in range(count - 1) if counts[i] < limit]
        whole, left = sum([loads[i] for i in movable]), surplus
        for i in movable:
            addition = min(limit - counts[i], max(1, left * loads[i] // whole), surplus)
            counts[i] = counts[i] + addition
            surplus = surplus - addition
    return np.array([limit] + counts)


def ragged_sizes(stream_key, count, total, most, slope):
    if count == 2:
        one = jax.random.randint(stream_key, (), max(1, total - most), min(most, total - 1) + 1)
        return jnp.stack([one, total - one])
    sizes = jnp.asarray(profile(count, total, most, slope), jnp.int32)
    twos = (count - 1) // 2
    source_of, taker = sizes[1:1 + 2 * twos:2], sizes[2:2 + 2 * twos:2]
    room = jnp.minimum(source_of - 1, most - taker)
    shifted = jax.random.randint(jax.random.fold_in(stream_key, 1), (twos,), 0, 1 << 20) % (room + 1)
    sizes = sizes.at[1:1 + 2 * twos:2].set(source_of - shifted).at[2:2 + 2 * twos:2].set(taker + shifted)
    return sizes[jax.random.permutation(jax.random.fold_in(stream_key, 2), count)]


def gaussian(own_key, dims, spread, most, split=(), held_as=jnp.bfloat16):
    array = jax.random.normal(own_key, dims, jnp.float32) * spread
    if len(split) > 0:
        array = block_levels(own_key, dims, split, -0.22, 0.18) * array
    return jnp.clip(array, min=-most, max=most).astype(held_as)


def setup_inputs(seed: int = 0) -> dict:
    arg_keys = jax.random.split(jax.random.key(seed), 5)
    return {
        "queries": draw_queries(jax.random.fold_in(arg_keys[4], 71), 0),
        "keys": draw_keys(jax.random.fold_in(arg_keys[4], 71), 0),
        "values": gaussian(arg_keys[2], (PACKED_TOKENS, KEY_VALUE_HEADS * HEAD_WIDTH), 1.0, 6.0, ((0, 128), (1, 4))),
        "doc_ids": jnp.searchsorted(jnp.cumsum(ragged_sizes(arg_keys[3], DOCS, PACKED_TOKENS, MAXDOC, 2)), jnp.arange(PACKED_TOKENS), side="right").astype(jnp.int32),
    }


def reference(queries, keys, values, doc_ids):
    seq_length = queries.shape[0]
    backward_extent = DOC_BLKS * BLOCK_TOKENS
    visible_span = backward_extent + BLOCK_TOKENS
    queries_per_group = QUERY_HEAD_COUNT // KEY_VALUE_HEADS
    score_scale = 1.0 / math.sqrt(HEAD_WIDTH)
    padded_key_rows = jnp.concatenate([jnp.zeros((backward_extent, KEY_VALUE_HEADS * HEAD_WIDTH), keys.dtype), keys], axis=0)
    padded_value_rows = jnp.concatenate([jnp.zeros((backward_extent, KEY_VALUE_HEADS * HEAD_WIDTH), values.dtype), values], axis=0)
    docs_padded = jnp.concatenate([-jnp.ones((backward_extent,), jnp.int32), doc_ids.astype(jnp.int32)], axis=0)

    def one_block(block_index):
        first_row = (block_index * BLOCK_TOKENS).astype(jnp.int32)
        block_of_queries = lax.dynamic_slice_in_dim(queries, first_row, BLOCK_TOKENS, 0)
        block_of_queries = block_of_queries.reshape(BLOCK_TOKENS, KEY_VALUE_HEADS, queries_per_group, HEAD_WIDTH).astype(jnp.float32)
        block_of_keys = lax.dynamic_slice_in_dim(padded_key_rows, first_row, visible_span, 0)
        block_of_keys = block_of_keys.reshape(visible_span, KEY_VALUE_HEADS, HEAD_WIDTH).astype(jnp.float32)
        block_of_values = lax.dynamic_slice_in_dim(padded_value_rows, first_row, visible_span, 0)
        block_of_values = block_of_values.reshape(visible_span, KEY_VALUE_HEADS, HEAD_WIDTH).astype(jnp.float32)
        query_docs = lax.dynamic_slice_in_dim(doc_ids.astype(jnp.int32), first_row, BLOCK_TOKENS, 0)
        key_docs = lax.dynamic_slice_in_dim(docs_padded, first_row, visible_span, 0)
        query_pos = first_row + jnp.arange(BLOCK_TOKENS, dtype=jnp.int32)
        key_pos = first_row - backward_extent + jnp.arange(visible_span, dtype=jnp.int32)
        allowed = (query_docs[:, None] == key_docs[None, :]) & (key_pos[None, :] <= query_pos[:, None])
        scores = jnp.einsum('qkgd,skd->kgqs', block_of_queries, block_of_keys) * score_scale
        scores = jnp.where(allowed, scores, -jnp.inf)
        rowmax = lax.optimization_barrier(jnp.max(scores, axis=-1, keepdims=True))
        weights = jnp.exp(scores - rowmax)
        denominator = lax.optimization_barrier(jnp.sum(weights, axis=-1))
        rounded = lax.optimization_barrier(weights.astype(jnp.bfloat16)).astype(jnp.float32)
        numerator = jnp.einsum('kgqs,skd->qkgd', rounded, block_of_values)
        result = numerator / jnp.transpose(denominator, (2, 0, 1))[..., None]
        return result.reshape(BLOCK_TOKENS, QUERY_HEAD_COUNT * HEAD_WIDTH).astype(jnp.bfloat16)
    blocks_out = lax.map(one_block, jnp.arange(seq_length // BLOCK_TOKENS, dtype=jnp.int32))
    return blocks_out.reshape(seq_length, QUERY_HEAD_COUNT * HEAD_WIDTH)
```

```python
import functools
import math

import jax
import jax.numpy as jnp
from jax import lax
from jax.experimental import pallas as pl
from jax.experimental.pallas import tpu as pltpu
from jax.sharding import PartitionSpec as P

HEAD_WIDTH = 128
DOC_ROWS = 16
MASKED = -1e30
SCORE_SCALE = math.log2(math.e) / math.sqrt(HEAD_WIDTH)


def shifted(value, steps):
    count = lax.axis_size("blk")
    return lax.ppermute(
        value, "blk", [(source, (source + steps) % count) for source in range(count)]
    )


def attend(n_packets, own, final, *refs):
    refs = list(refs)
    q_ref, doc_ref = refs[:2]
    packets = refs[2 : 2 + n_packets]
    rest = refs[2 + n_packets :]
    if own:
        prev = None
    else:
        prev, rest = rest[:2], rest[2:]
    rows = q_ref.shape[0]
    kv_cols = packets[0].shape[1] // 2
    kv_heads = kv_cols // HEAD_WIDTH
    q_heads = q_ref.shape[1] // HEAD_WIDTH
    group = q_heads // kv_heads
    q_docs = doc_ref[...]
    biases = []
    for number, packet in enumerate(packets):
        key_docs = packet[rows : rows + DOC_ROWS, :rows].astype(jnp.float32)[0:1, :]
        allowed = q_docs == key_docs
        if own and number == 0:
            row = lax.broadcasted_iota(jnp.int32, (rows, rows), 0)
            col = lax.broadcasted_iota(jnp.int32, (rows, rows), 1)
            allowed = allowed & (col <= row)
        biases.append(jnp.where(allowed, 0.0, MASKED).astype(jnp.float32))
    for head in range(q_heads):
        kv = head // group
        lanes = slice(head * HEAD_WIDTH, (head + 1) * HEAD_WIDTH)
        q = q_ref[:, lanes]
        scores = []
        top = None
        for packet, bias in zip(packets, biases):
            k = packet[:rows, kv * HEAD_WIDTH : (kv + 1) * HEAD_WIDTH]
            s = lax.dot_general(
                q, k, (((1,), (1,)), ((), ())), preferred_element_type=jnp.float32
            )
            s = s * SCORE_SCALE + bias
            scores.append(s)
            m = jnp.max(s, axis=1, keepdims=True)
            top = m if top is None else jnp.maximum(top, m)
        if prev is not None:
            old_top = prev[1][:, head : head + 1]
            old_den = prev[1][:, q_heads + head : q_heads + head + 1]
            top = jnp.maximum(top, old_top)
            fade = jnp.exp2(old_top - top)
            den = old_den * fade
            num = prev[0][:, lanes] * fade
        else:
            den = num = None
        for packet, s in zip(packets, scores):
            v = packet[:rows, kv_cols + kv * HEAD_WIDTH : kv_cols + (kv + 1) * HEAD_WIDTH]
            w = jnp.exp2(s - top)
            part = jnp.sum(w, axis=1, keepdims=True)
            add = jnp.dot(w.astype(jnp.bfloat16), v, preferred_element_type=jnp.float32)
            den = part if den is None else den + part
            num = add if num is None else num + add
        if final:
            rest[0][:, lanes] = (num * (1.0 / den)).astype(jnp.bfloat16)
        else:
            rest[0][:, lanes] = num
            rest[1][:, head : head + 1] = top
            rest[1][:, q_heads + head : q_heads + head + 1] = den


def fold(queries, q_docs, packets, state, final):
    rows, cols = queries.shape
    q_heads = cols // HEAD_WIDTH
    if final:
        out_shape = jax.ShapeDtypeStruct((rows, cols), jnp.bfloat16)
    else:
        out_shape = (
            jax.ShapeDtypeStruct((rows, cols), jnp.float32),
            jax.ShapeDtypeStruct((rows, 2 * q_heads), jnp.float32),
        )
    args = [queries, q_docs, *packets, *(state or ())]
    work = len(packets) * rows * rows * q_heads
    return pl.pallas_call(
        functools.partial(attend, len(packets), state is None, final),
        out_shape=out_shape,
        compiler_params=pltpu.CompilerParams(vmem_limit_bytes=32 * 1024 * 1024),
        cost_estimate=pl.CostEstimate(
            flops=4 * work * HEAD_WIDTH, bytes_accessed=3 * rows * cols, transcendentals=work
        ),
    )(*args)


def shards(queries, keys, values, doc_ids):
    rows = queries.shape[0]
    docs = doc_ids + 1
    doc_rows = jnp.broadcast_to(docs.astype(jnp.bfloat16)[None, :], (DOC_ROWS, rows))
    doc_rows = jnp.concatenate([doc_rows, doc_rows], axis=1)
    packet = jnp.concatenate([jnp.concatenate([keys, values], axis=1), doc_rows], axis=0)
    q_docs = docs.astype(jnp.float32)[:, None]

    one = shifted(packet, 1)
    four = shifted(packet, 4)
    two = shifted(one, 1)
    three = shifted(four, -1)

    state = fold(queries, q_docs, [packet], None, False)
    state = fold(queries, q_docs, [one], state, False)
    state = fold(queries, q_docs, [four], state, False)
    return fold(queries, q_docs, [two, three], state, True)


def solution(mesh):
    return jax.shard_map(
        shards,
        mesh=mesh,
        in_specs=(P("blk", "heads"), P("blk", "heads"), P("blk", "heads"), P("blk")),
        out_specs=P("blk", "heads"),
        check_vma=False,
    )
```

```python
import functools
import math

import jax
import jax.numpy as jnp
from jax import lax
from jax.experimental import pallas as pl
from jax.experimental.pallas import tpu as pltpu
from jax.sharding import PartitionSpec as P

HEAD_WIDTH = 128
DOC_ROWS = 16
MASKED = -1e30
SCORE_SCALE = math.log2(math.e) / math.sqrt(HEAD_WIDTH)


def shifted(value, steps, kept=lambda source: True):
    count = lax.axis_size("blk")
    pairs = [(source, source + steps) for source in range(count) if 0 <= source + steps < count]
    return lax.ppermute(value, "blk", [pair for pair in pairs if kept(pair[0])])


def summed(refs, index):
    total = refs[0][index]
    for ref in refs[1:]:
        total = total + ref[index]
    return total


def attend(counts, own, final, *refs):
    refs = list(refs)
    q_ref, doc_ref = refs[:2]
    rest = refs[2:]
    packets = []
    for count in counts:
        packets.append(rest[:count])
        rest = rest[count:]
    if own:
        prev = None
    else:
        prev, rest = rest[:3], rest[3:]
    rows = q_ref.shape[0]
    kv_cols = packets[0][0].shape[1] // 2
    kv_heads = kv_cols // HEAD_WIDTH
    q_heads = q_ref.shape[1] // HEAD_WIDTH
    group = q_heads // kv_heads
    q_docs = doc_ref[...]
    biases = []
    for number, packet in enumerate(packets):
        key_docs = summed(packet, (slice(rows, rows + DOC_ROWS), slice(0, rows)))
        key_docs = key_docs.astype(jnp.float32)[0:1, :]
        allowed = q_docs == key_docs
        if own and number == 0:
            row = lax.broadcasted_iota(jnp.int32, (rows, rows), 0)
            col = lax.broadcasted_iota(jnp.int32, (rows, rows), 1)
            allowed = allowed & (col <= row)
        biases.append(jnp.where(allowed, 0.0, MASKED).astype(jnp.float32))
    copies = []
    for head in range(q_heads):
        kv = head // group
        lanes = slice(head * HEAD_WIDTH, (head + 1) * HEAD_WIDTH)
        q = q_ref[:, lanes]
        scores = []
        top = None
        for packet, bias in zip(packets, biases):
            k = summed(packet, (slice(0, rows), slice(kv * HEAD_WIDTH, (kv + 1) * HEAD_WIDTH)))
            s = lax.dot_general(
                q, k, (((1,), (1,)), ((), ())), preferred_element_type=jnp.float32
            )
            s = s * SCORE_SCALE + bias
            scores.append(s)
            m = jnp.max(s, axis=1, keepdims=True)
            top = m if top is None else jnp.maximum(top, m)
        top = jnp.broadcast_to(top, (rows, HEAD_WIDTH))
        if prev is not None:
            old_top = prev[1][:, lanes]
            top = jnp.maximum(top, old_top)
            fade = jnp.exp2(old_top - top)
            den = prev[2][:, lanes] * fade
            num = prev[0][:, lanes] * fade
        else:
            den = num = None
        wide_top = jnp.concatenate([top] * (rows // HEAD_WIDTH), axis=1)
        for packet, s in zip(packets, scores):
            first = kv_cols + kv * HEAD_WIDTH
            v = summed(packet, (slice(0, rows), slice(first, first + HEAD_WIDTH)))
            w = jnp.exp2(s - wide_top)
            part = jnp.broadcast_to(jnp.sum(w, axis=1, keepdims=True), (rows, HEAD_WIDTH))
            add = jnp.dot(w.astype(jnp.bfloat16), v, preferred_element_type=jnp.float32)
            den = part if den is None else den + part
            num = add if num is None else num + add
        if final:
            out_ref, held, sems = rest
            held[:, lanes] = (num * (1.0 / den)).astype(jnp.bfloat16)
            copies.append(
                pltpu.make_async_copy(held.at[:, lanes], out_ref.at[:, lanes], sems.at[head])
            )
            copies[-1].start()
        else:
            rest[0][:, lanes] = num
            rest[1][:, lanes] = top
            rest[2][:, lanes] = den
    for copy in copies:
        copy.wait()


def fold(queries, q_docs, packets, state, final):
    rows, cols = queries.shape
    q_heads = cols // HEAD_WIDTH
    extra = {}
    if final:
        out_shape = jax.ShapeDtypeStruct((rows, cols), jnp.bfloat16)
        extra = dict(
            out_specs=pl.BlockSpec(memory_space=pltpu.HBM),
            scratch_shapes=[
                pltpu.VMEM((rows, cols), jnp.bfloat16),
                pltpu.SemaphoreType.DMA((q_heads,)),
            ],
        )
    else:
        out_shape = (jax.ShapeDtypeStruct((rows, cols), jnp.float32),) * 3
    args = [queries, q_docs, *[part for packet in packets for part in packet], *(state or ())]
    work = len(packets) * rows * rows * q_heads
    return pl.pallas_call(
        functools.partial(attend, [len(packet) for packet in packets], state is None, final),
        out_shape=out_shape,
        **extra,
        compiler_params=pltpu.CompilerParams(vmem_limit_bytes=32 * 1024 * 1024),
        cost_estimate=pl.CostEstimate(
            flops=4 * work * HEAD_WIDTH, bytes_accessed=3 * rows * cols, transcendentals=work
        ),
    )(*args)


def pack(keys, values, doc_ids):
    rows = keys.shape[0]
    docs = jnp.broadcast_to(doc_ids[None, :], (DOC_ROWS, rows))
    docs = lax.optimization_barrier(docs)
    docs = (docs + 1).astype(keys.dtype)
    return jnp.concatenate(
        [jnp.concatenate([keys, docs], axis=0), jnp.concatenate([values, docs], axis=0)], axis=1
    )


def shards(queries, keys, values, doc_ids):
    packet = pack(keys, values, doc_ids)
    q_docs = (doc_ids + 1).astype(jnp.float32)[:, None]
    count = lax.axis_size("blk")

    one = shifted(packet, 1)
    four = shifted(packet, 4)
    last_three = shifted(packet, 3, lambda source: source == count - 4)
    state = fold(queries, q_docs, [[packet]], None, False)
    one, state = lax.optimization_barrier((one, state))
    two = shifted(one, 1)
    state = fold(queries, q_docs, [[one]], state, False)
    four, last_three, state = lax.optimization_barrier((four, last_three, state))
    three = shifted(four, -1)
    state = fold(queries, q_docs, [[four]], state, False)
    state = fold(queries, q_docs, [[two]], state, False)
    return fold(queries, q_docs, [[three, last_three]], state, True)


def solution(mesh):
    return jax.shard_map(
        shards,
        mesh=mesh,
        in_specs=(P("blk", "heads"), P("blk", "heads"), P("blk", "heads"), P("blk")),
        out_specs=P("blk", "heads"),
        check_vma=False,
    )
```

```python
import functools
import math

import jax
import jax.numpy as jnp
from jax import lax
from jax.experimental import pallas as pl
from jax.experimental.pallas import tpu as pltpu
from jax.sharding import PartitionSpec as P

HEAD_WIDTH = 128
DOC_ROWS = 8
PLANE = 32
MASKED = -1e30
SCORE_SCALE = math.log2(math.e) / math.sqrt(HEAD_WIDTH)


def shifted(value, steps, kept=lambda source: True):
    count = lax.axis_size("blk")
    pairs = [(source, source + steps) for source in range(count) if 0 <= source + steps < count]
    return lax.ppermute(value, "blk", [pair for pair in pairs if kept(pair[0])])


def summed(refs, index):
    total = refs[0][index]
    for ref in refs[1:]:
        total = total + ref[index]
    return total


def attend(counts, own, final, *refs):
    refs = list(refs)
    q_ref, doc_ref = refs[:2]
    rest = refs[2:]
    packets = []
    for count in counts:
        packets.append(rest[:count])
        rest = rest[count:]
    if own:
        prev = None
    else:
        prev, rest = rest[:3], rest[3:]
    rows = q_ref.shape[0]
    kv_cols = packets[0][0].shape[1] // 2
    kv_heads = kv_cols // HEAD_WIDTH
    q_heads = q_ref.shape[1] // HEAD_WIDTH
    group = q_heads // kv_heads
    q_docs = doc_ref[...]
    biases = []
    for number, packet in enumerate(packets):
        key_docs = summed(packet, (slice(rows, rows + DOC_ROWS), slice(0, rows)))
        key_docs = key_docs.astype(jnp.float32)[0:1, :]
        allowed = q_docs == key_docs
        if own and number == 0:
            row = lax.broadcasted_iota(jnp.int32, (rows, rows), 0)
            col = lax.broadcasted_iota(jnp.int32, (rows, rows), 1)
            allowed = allowed & (col <= row)
        biases.append(jnp.where(allowed, 0.0, MASKED).astype(jnp.float32))
    copies = []
    for head in range(q_heads):
        kv = head // group
        lanes = slice(head * HEAD_WIDTH, (head + 1) * HEAD_WIDTH)
        q = q_ref[:, lanes]
        scores = []
        top = None
        for packet, bias in zip(packets, biases):
            k = summed(packet, (slice(0, rows), slice(kv * HEAD_WIDTH, (kv + 1) * HEAD_WIDTH)))
            s = lax.dot_general(
                q, k, (((1,), (1,)), ((), ())), preferred_element_type=jnp.float32
            )
            s = s * SCORE_SCALE + bias
            scores.append(s)
            m = jnp.max(s, axis=1, keepdims=True)
            top = m if top is None else jnp.maximum(top, m)
        top = jnp.broadcast_to(top, (rows, HEAD_WIDTH))
        if prev is not None:
            old_top = prev[1][:, lanes]
            top = jnp.maximum(top, old_top)
            fade = jnp.exp2(old_top - top)
            den = prev[2][:, lanes] * fade
            num = prev[0][:, lanes] * fade
        else:
            den = num = None
        wide_top = jnp.concatenate([top] * (rows // HEAD_WIDTH), axis=1)
        for packet, s in zip(packets, scores):
            first = kv_cols + kv * HEAD_WIDTH
            v = summed(packet, (slice(0, rows), slice(first, first + HEAD_WIDTH)))
            w = jnp.exp2(s - wide_top).astype(jnp.bfloat16)
            v = jnp.concatenate([v, jnp.ones_like(v)], axis=1)
            both = jnp.dot(w, v, preferred_element_type=jnp.float32)
            add, part = both[:, :HEAD_WIDTH], both[:, HEAD_WIDTH:]
            den = part if den is None else den + part
            num = add if num is None else num + add
        if final:
            out_ref, held, sems = rest
            held[:, lanes] = (num * (1.0 / den)).astype(jnp.bfloat16)
            copies.append(
                pltpu.make_async_copy(held.at[:, lanes], out_ref.at[:, lanes], sems.at[head])
            )
            copies[-1].start()
        else:
            rest[0][:, lanes] = num
            rest[1][:, lanes] = top
            rest[2][:, lanes] = den
    for copy in copies:
        copy.wait()


def fold(queries, q_docs, packets, state, final):
    rows, cols = queries.shape
    q_heads = cols // HEAD_WIDTH
    extra = {}
    if final:
        out_shape = jax.ShapeDtypeStruct((rows, cols), jnp.bfloat16)
        extra = dict(
            out_specs=pl.BlockSpec(memory_space=pltpu.HBM),
            scratch_shapes=[
                pltpu.VMEM((rows, cols), jnp.bfloat16),
                pltpu.SemaphoreType.DMA((q_heads,)),
            ],
        )
    else:
        out_shape = (jax.ShapeDtypeStruct((rows, cols), jnp.float32),) * 3
    args = [queries, q_docs, *[part for packet in packets for part in packet], *(state or ())]
    work = len(packets) * rows * rows * q_heads
    return pl.pallas_call(
        functools.partial(attend, [len(packet) for packet in packets], state is None, final),
        out_shape=out_shape,
        **extra,
        compiler_params=pltpu.CompilerParams(vmem_limit_bytes=32 * 1024 * 1024),
        cost_estimate=pl.CostEstimate(
            flops=4 * work * HEAD_WIDTH, bytes_accessed=3 * rows * cols, transcendentals=work
        ),
    )(*args)


def pack(keys, values, doc_ids):
    rows, cols = keys.shape
    packet = jnp.concatenate([keys, values], axis=1)
    packet = jnp.pad(packet, ((0, DOC_ROWS), (0, 0)))
    packet, doc_ids = lax.optimization_barrier((packet, doc_ids))
    docs = jnp.broadcast_to((doc_ids + 1).astype(keys.dtype)[None, :], (DOC_ROWS, rows))
    return lax.dynamic_update_slice(packet, docs, (rows, 0))


def shards(queries, keys, values, doc_ids):
    packet = pack(keys, values, doc_ids)
    q_docs = (doc_ids + 1).astype(jnp.float32)[:, None]

    far = lambda source: source % PLANE == PLANE - 4
    one = shifted(packet, 1)
    four = shifted(packet, 4, lambda source: not far(source))
    far_four = shifted(packet, 4, far)
    far_three = shifted(packet, 3, far)
    two = shifted(one, 1)
    three = shifted(four, -1, lambda source: source % PLANE != 0)
    state = fold(queries, q_docs, [[packet]], None, False)
    state = fold(queries, q_docs, [[one]], state, False)
    state = fold(queries, q_docs, [[four, far_four]], state, False)
    state = fold(queries, q_docs, [[two]], state, False)
    return fold(queries, q_docs, [[three, far_three]], state, True)


def solution(mesh):
    return jax.shard_map(
        shards,
        mesh=mesh,
        in_specs=(P("blk", "heads"), P("blk", "heads"), P("blk", "heads"), P("blk")),
        out_specs=P("blk", "heads"),
        check_vma=False,
    )
```

```python
import functools
import math

import jax
import jax.numpy as jnp
from jax import lax
from jax.experimental import pallas as pl
from jax.experimental.pallas import tpu as pltpu
from jax.sharding import PartitionSpec as P

HEAD_WIDTH = 128
DOC_ROWS = 8
PLANE = 32
MASKED = -1e30
SCORE_SCALE = math.log2(math.e) / math.sqrt(HEAD_WIDTH)


def shifted(value, steps, kept=lambda source: True):
    count = lax.axis_size("blk")
    pairs = [(source, source + steps) for source in range(count) if 0 <= source + steps < count]
    return lax.ppermute(value, "blk", [pair for pair in pairs if kept(pair[0])])


def summed(refs, index):
    total = refs[0][index]
    for ref in refs[1:]:
        total = total + ref[index]
    return total


def attend(counts, own, final, *refs):
    refs = list(refs)
    q_ref, doc_ref = refs[:2]
    rest = refs[2:]
    packets = []
    for count in counts:
        packets.append(rest[:count])
        rest = rest[count:]
    if own:
        prev = None
    else:
        prev, rest = rest[:3], rest[3:]
    rows = q_ref.shape[0]
    kv_cols = packets[0][0].shape[1] // 2
    kv_heads = kv_cols // HEAD_WIDTH
    q_heads = q_ref.shape[1] // HEAD_WIDTH
    group = q_heads // kv_heads
    q_docs = doc_ref[...]
    biases = []
    for number, packet in enumerate(packets):
        key_docs = summed(packet, (slice(rows, rows + DOC_ROWS), slice(0, rows)))
        key_docs = key_docs.astype(jnp.float32)[0:1, :]
        allowed = q_docs == key_docs
        if own and number == 0:
            row = lax.broadcasted_iota(jnp.int32, (rows, rows), 0)
            col = lax.broadcasted_iota(jnp.int32, (rows, rows), 1)
            allowed = allowed & (col <= row)
        biases.append(jnp.where(allowed, 0.0, MASKED).astype(jnp.float32))
    copies = []
    stacked = group * rows
    for kv in range(kv_heads):
        heads = range(kv * group, (kv + 1) * group)
        span = slice(kv * stacked, (kv + 1) * stacked)
        q = jnp.concatenate([q_ref[:, h * HEAD_WIDTH : (h + 1) * HEAD_WIDTH] for h in heads], axis=0)
        scores = []
        top = None
        for packet, bias in zip(packets, biases):
            k = summed(packet, (slice(0, rows), slice(kv * HEAD_WIDTH, (kv + 1) * HEAD_WIDTH)))
            s = lax.dot_general(
                q, k, (((1,), (1,)), ((), ())), preferred_element_type=jnp.float32
            )
            s = s.reshape(group, rows, rows) * SCORE_SCALE + bias[None]
            s = s.reshape(stacked, rows)
            scores.append(s)
            m = jnp.max(s, axis=1, keepdims=True)
            top = m if top is None else jnp.maximum(top, m)
        top = jnp.broadcast_to(top, (stacked, HEAD_WIDTH))
        if prev is not None:
            old_top = prev[1][span, :]
            top = jnp.maximum(top, old_top)
            fade = jnp.exp2(old_top - top)
            den = prev[2][span, :] * fade
            num = prev[0][span, :] * fade
        else:
            den = num = None
        wide_top = jnp.concatenate([top] * (rows // HEAD_WIDTH), axis=1)
        for packet, s in zip(packets, scores):
            first = kv_cols + kv * HEAD_WIDTH
            v = summed(packet, (slice(0, rows), slice(first, first + HEAD_WIDTH)))
            w = jnp.exp2(s - wide_top).astype(jnp.bfloat16)
            v = jnp.concatenate([v, jnp.ones_like(v)], axis=1)
            both = jnp.dot(w, v, preferred_element_type=jnp.float32)
            add, part = both[:, :HEAD_WIDTH], both[:, HEAD_WIDTH:]
            den = part if den is None else den + part
            num = add if num is None else num + add
        if final:
            out_ref, held, sems = rest
            done = (num * (1.0 / den)).astype(jnp.bfloat16)
            for place, head in enumerate(heads):
                lanes = slice(head * HEAD_WIDTH, (head + 1) * HEAD_WIDTH)
                held[:, lanes] = done[place * rows : (place + 1) * rows]
                copies.append(
                    pltpu.make_async_copy(held.at[:, lanes], out_ref.at[:, lanes], sems.at[head])
                )
                copies[-1].start()
        else:
            rest[0][span, :] = num
            rest[1][span, :] = top
            rest[2][span, :] = den
    for copy in copies:
        copy.wait()


def fold(queries, q_docs, packets, state, final):
    rows, cols = queries.shape
    q_heads = cols // HEAD_WIDTH
    extra = {}
    if final:
        out_shape = jax.ShapeDtypeStruct((rows, cols), jnp.bfloat16)
        extra = dict(
            out_specs=pl.BlockSpec(memory_space=pltpu.HBM),
            scratch_shapes=[
                pltpu.VMEM((rows, cols), jnp.bfloat16),
                pltpu.SemaphoreType.DMA((q_heads,)),
            ],
        )
    else:
        out_shape = (jax.ShapeDtypeStruct((rows * q_heads, HEAD_WIDTH), jnp.float32),) * 3
    args = [queries, q_docs, *[part for packet in packets for part in packet], *(state or ())]
    work = len(packets) * rows * rows * q_heads
    return pl.pallas_call(
        functools.partial(attend, [len(packet) for packet in packets], state is None, final),
        out_shape=out_shape,
        **extra,
        compiler_params=pltpu.CompilerParams(vmem_limit_bytes=32 * 1024 * 1024),
        cost_estimate=pl.CostEstimate(
            flops=4 * work * HEAD_WIDTH, bytes_accessed=3 * rows * cols, transcendentals=work
        ),
    )(*args)


def pack(keys, values, doc_ids):
    rows, cols = keys.shape
    packet = jnp.concatenate([keys, values], axis=1)
    packet = jnp.pad(packet, ((0, DOC_ROWS), (0, 0)))
    packet, doc_ids = lax.optimization_barrier((packet, doc_ids))
    docs = jnp.broadcast_to((doc_ids + 1).astype(keys.dtype)[None, :], (DOC_ROWS, rows))
    return lax.dynamic_update_slice(packet, docs, (rows, 0))


def shards(queries, keys, values, doc_ids):
    packet = pack(keys, values, doc_ids)
    q_docs = (doc_ids + 1).astype(jnp.float32)[:, None]

    far = lambda source: source % PLANE == PLANE - 4
    one = shifted(packet, 1)
    four = shifted(packet, 4, lambda source: not far(source))
    far_four = shifted(packet, 4, far)
    far_three = shifted(packet, 3, far)
    two = shifted(one, 1)
    three = shifted(four, -1, lambda source: source % PLANE != 0)
    state = fold(queries, q_docs, [[packet]], None, False)
    state = fold(queries, q_docs, [[one]], state, False)
    state = fold(queries, q_docs, [[four, far_four]], state, False)
    state = fold(queries, q_docs, [[two]], state, False)
    return fold(queries, q_docs, [[three, far_three]], state, True)


def solution(mesh):
    return jax.shard_map(
        shards,
        mesh=mesh,
        in_specs=(P("blk", "heads"), P("blk", "heads"), P("blk", "heads"), P("blk")),
        out_specs=P("blk", "heads"),
        check_vma=False,
    )
```

```python
import functools
import math

import jax
import jax.numpy as jnp
from jax import lax
from jax.experimental import pallas as pl
from jax.experimental.pallas import tpu as pltpu
from jax.sharding import PartitionSpec as P

HEAD_WIDTH = 128
DOC_ROWS = 8
PLANE = 32
MASKED = -1e30
SCORE_SCALE = math.log2(math.e) / math.sqrt(HEAD_WIDTH)


def shifted(value, steps, kept=lambda source: True):
    count = lax.axis_size("blk")
    pairs = [(source, source + steps) for source in range(count) if 0 <= source + steps < count]
    return lax.ppermute(value, "blk", [pair for pair in pairs if kept(pair[0])])


def summed(refs, index):
    total = refs[0][index]
    for ref in refs[1:]:
        total = total + ref[index]
    return total


def attend(counts, own, final, *refs):
    refs = list(refs)
    q_ref, doc_ref = refs[:2]
    rest = refs[2:]
    packets = []
    for count in counts:
        packets.append(rest[:count])
        rest = rest[count:]
    if own:
        prev = None
    else:
        prev, rest = rest[:3], rest[3:]
    rows = q_ref.shape[0]
    kv_cols = packets[0][0].shape[1] // 2
    kv_heads = kv_cols // HEAD_WIDTH
    q_heads = q_ref.shape[1] // HEAD_WIDTH
    group = q_heads // kv_heads
    q_docs = doc_ref[...]
    biases = []
    for number, packet in enumerate(packets):
        key_docs = summed(packet, (slice(rows, rows + DOC_ROWS), slice(0, rows)))
        key_docs = key_docs.astype(jnp.float32)[0:1, :]
        allowed = q_docs == key_docs
        if own and number == 0:
            row = lax.broadcasted_iota(jnp.int32, (rows, rows), 0)
            col = lax.broadcasted_iota(jnp.int32, (rows, rows), 1)
            allowed = allowed & (col <= row)
        biases.append(jnp.where(allowed, 0.0, MASKED).astype(jnp.float32))
    copies = []
    step = group // 2 if final and group % 2 == 0 else group
    stacked = step * rows
    for start in range(0, q_heads, step):
        kv = start // group
        heads = range(start, start + step)
        span = slice(start * rows, (start + step) * rows)
        q = jnp.concatenate([q_ref[:, h * HEAD_WIDTH : (h + 1) * HEAD_WIDTH] for h in heads], axis=0)
        scores = []
        top = None
        for packet, bias in zip(packets, biases):
            k = summed(packet, (slice(0, rows), slice(kv * HEAD_WIDTH, (kv + 1) * HEAD_WIDTH)))
            s = lax.dot_general(
                q, k, (((1,), (1,)), ((), ())), preferred_element_type=jnp.float32
            )
            s = s.reshape(step, rows, rows) * SCORE_SCALE + bias[None]
            s = s.reshape(stacked, rows)
            scores.append(s)
            m = jnp.max(s, axis=1, keepdims=True)
            top = m if top is None else jnp.maximum(top, m)
        top = jnp.broadcast_to(top, (stacked, HEAD_WIDTH))
        if prev is not None:
            old_top = prev[1][span, :]
            top = jnp.maximum(top, old_top)
            fade = jnp.exp2(old_top - top)
            den = prev[2][span, :] * fade
            num = prev[0][span, :] * fade
        else:
            den = num = None
        wide_top = jnp.concatenate([top] * (rows // HEAD_WIDTH), axis=1)
        for packet, s in zip(packets, scores):
            first = kv_cols + kv * HEAD_WIDTH
            v = summed(packet, (slice(0, rows), slice(first, first + HEAD_WIDTH)))
            w = jnp.exp2(s - wide_top).astype(jnp.bfloat16)
            v = jnp.concatenate([v, jnp.ones_like(v)], axis=1)
            both = jnp.dot(w, v, preferred_element_type=jnp.float32)
            add, part = both[:, :HEAD_WIDTH], both[:, HEAD_WIDTH:]
            den = part if den is None else den + part
            num = add if num is None else num + add
        if final:
            out_ref, held, sems = rest
            done = (num * (1.0 / den)).astype(jnp.bfloat16)
            for place, head in enumerate(heads):
                lanes = slice(head * HEAD_WIDTH, (head + 1) * HEAD_WIDTH)
                held[:, lanes] = done[place * rows : (place + 1) * rows]
                copies.append(
                    pltpu.make_async_copy(held.at[:, lanes], out_ref.at[:, lanes], sems.at[head])
                )
                copies[-1].start()
        else:
            rest[0][span, :] = num
            rest[1][span, :] = top
            rest[2][span, :] = den
    for copy in copies:
        copy.wait()


def fold(queries, q_docs, packets, state, final):
    rows, cols = queries.shape
    q_heads = cols // HEAD_WIDTH
    extra = {}
    if final:
        out_shape = jax.ShapeDtypeStruct((rows, cols), jnp.bfloat16)
        extra = dict(
            out_specs=pl.BlockSpec(memory_space=pltpu.HBM),
            scratch_shapes=[
                pltpu.VMEM((rows, cols), jnp.bfloat16),
                pltpu.SemaphoreType.DMA((q_heads,)),
            ],
        )
    else:
        out_shape = (jax.ShapeDtypeStruct((rows * q_heads, HEAD_WIDTH), jnp.float32),) * 3
    args = [queries, q_docs, *[part for packet in packets for part in packet], *(state or ())]
    work = len(packets) * rows * rows * q_heads
    return pl.pallas_call(
        functools.partial(attend, [len(packet) for packet in packets], state is None, final),
        out_shape=out_shape,
        **extra,
        compiler_params=pltpu.CompilerParams(vmem_limit_bytes=32 * 1024 * 1024),
        cost_estimate=pl.CostEstimate(
            flops=4 * work * HEAD_WIDTH, bytes_accessed=3 * rows * cols, transcendentals=work
        ),
    )(*args)


def pack(keys, values, doc_ids):
    rows, cols = keys.shape
    packet = jnp.concatenate([keys, values], axis=1)
    packet = jnp.pad(packet, ((0, DOC_ROWS), (0, 0)))
    packet, doc_ids = lax.optimization_barrier((packet, doc_ids))
    docs = jnp.broadcast_to((doc_ids + 1).astype(keys.dtype)[None, :], (DOC_ROWS, rows))
    return lax.dynamic_update_slice(packet, docs, (rows, 0))


def shards(queries, keys, values, doc_ids):
    packet = pack(keys, values, doc_ids)
    q_docs = (doc_ids + 1).astype(jnp.float32)[:, None]

    far = lambda source: source % PLANE == PLANE - 4
    one = shifted(packet, 1)
    four = shifted(packet, 4, lambda source: not far(source))
    far_four = shifted(packet, 4, far)
    far_three = shifted(packet, 3, far)
    two = shifted(one, 1)
    three = shifted(four, -1, lambda source: source % PLANE != 0)
    state = fold(queries, q_docs, [[packet]], None, False)
    state = fold(queries, q_docs, [[one]], state, False)
    state = fold(queries, q_docs, [[four], [far_four, far_three]], state, False)
    state = fold(queries, q_docs, [[two]], state, False)
    return fold(queries, q_docs, [[three]], state, True)


def solution(mesh):
    return jax.shard_map(
        shards,
        mesh=mesh,
        in_specs=(P("blk", "heads"), P("blk", "heads"), P("blk", "heads"), P("blk")),
        out_specs=P("blk", "heads"),
        check_vma=False,
    )
```
